32 devices in a mesh: mem: 2 (over x), tx: 4 (over z), ty: 4 (over y, core).
Axes of the slice: x: 2, y: 2, z: 4, core: 2. Of those that a mesh axis runs over, the one named last changes fastest.
Arguments:
- pressure: float32 [16, 1024, 1024], P('mem', 'tx', 'ty'), may hold values from -6 to 6
- elevation: float32 [1024, 1024], P('tx', 'ty'), may hold values from -4 to 4
- ks_field: float32 [1024, 1024], P('tx', 'ty'), may hold values from 0.03 to 0.24
- melt_rate: float32 [16, 1024, 1024], P('mem', 'tx', 'ty'), may hold values from -1.5 to 1.5
- obs_index: int32 [1024], replicated, may hold values from 0 to 1048575
- obs_value: float32 [1024], P(('tx', 'ty')), may hold values from -6 to 6
- obs_error: float32 [1024], P(('tx', 'ty')), may hold values from 0.3 to 1
- perturbation: float32 [1024, 16], P(('tx', 'ty'), 'mem'), may hold values from -6 to 6
Outputs:
- analysis: float32 [16, 1024, 1024], P('mem', 'tx', 'ty')
The draws below stay inside these ranges and needn't reach their ends.
All inputs are finite; a program needn't handle non-finite values.
Results may differ from the reference program's by a relative error of at most 0.0089.
Values may be sent and summed in bfloat16 or wider, within the bound.
A program may use at most 128 MiB of HBM per device.

```python
import math
import jax
import jax.numpy as jnp
from jax import lax

MEM_DEV = 8
NOBS = 1024
SUBSTEPS = 4
NODES_ACROSS = 1024
NODES_DOWNSLOPE = 1024
REPLICA_COUNT = 16
N_MEM = 2


def touch_ends(array, stream_key, smallest, high):
    index_at = [jax.random.randint(jax.random.fold_in(stream_key, axis), (), 0, length) for axis, length in enumerate(array.shape)]
    longest = array.shape.index(max(array.shape))
    beside = index_at[:longest] + [(index_at[longest] + 1) % array.shape[longest]] + index_at[longest + 1:]
    return array.at[tuple(index_at)].set(smallest).at[tuple(beside)].set(high)


def block_levels(key, dims, pieces, least, largest):
    def one(axis_at, parts):
        heights = jax.random.uniform(jax.random.fold_in(jax.random.fold_in(key, 6), axis_at), (parts,), jnp.float32, least / len(pieces), largest / len(pieces))
        return jnp.repeat(jnp.exp(heights), dims[axis_at] // parts).reshape((-1,) + (1,) * (len(dims) - axis_at - 1))

    loudness = one(*pieces[0])
    for cut in pieces[1:]:
        loudness = loudness * one(*cut)
    return loudness


def noise(own_key, extent, deviation, limit, shards=(), kind=jnp.bfloat16):
    level = block_levels(own_key, extent, shards, -0.22, 0.18) if shards else 1.0
    entries = jax.random.normal(own_key, extent, jnp.float32) * deviation * level
    return jnp.minimum(jnp.maximum(entries, -limit), limit).astype(kind)


def setup_inputs(seed: int = 0) -> dict:
    streams_of = jax.random.split(jax.random.key(seed), 9)
    pressure = noise(streams_of[0], (REPLICA_COUNT, NODES_ACROSS, NODES_DOWNSLOPE), 1.0, 6.0, ((0, 2), (1, 4), (2, 4)), jnp.float32)
    elevation = noise(streams_of[1], (NODES_ACROSS, NODES_DOWNSLOPE), 0.5, 4.0, ((0, 4), (1, 4)), jnp.float32)
    ks_field = jnp.clip(jnp.exp(math.log(0.24) - 2.0794415 * jax.random.uniform(streams_of[2], (NODES_ACROSS, NODES_DOWNSLOPE), jnp.float32) ** block_levels(streams_of[2], (NODES_ACROSS, NODES_DOWNSLOPE), ((0, 4), (1, 4)), -0.2, 0.2)), 0.03, 0.24)
    melt_rate = noise(streams_of[3], (REPLICA_COUNT, NODES_ACROSS, NODES_DOWNSLOPE), 0.25, 1.5, ((0, 2), (1, 4), (2, 4)), jnp.float32)
    obs_index = touch_ends(jax.random.randint(streams_of[4], (NOBS,), 0, NODES_ACROSS * NODES_DOWNSLOPE), jax.random.fold_in(streams_of[4], 1), 0, (NODES_ACROSS * NODES_DOWNSLOPE) - 1).astype(jnp.int32)
    obs_value = noise(streams_of[5], (NOBS,), 1.0, 6.0, ((0, 16),), jnp.float32)
    obs_error = jnp.clip(jnp.exp(math.log(1.0) - 1.2039728 * jax.random.uniform(streams_of[6], (NOBS,), jnp.float32) ** block_levels(streams_of[6], (NOBS,), ((0, 16),), -0.2, 0.2)), 0.3, 1.0)
    perturbation = noise(streams_of[7], (NOBS, REPLICA_COUNT), 1.0, 6.0, ((0, 16), (1, 2)), jnp.float32)
    return {"pressure": pressure, "elevation": elevation, "ks_field": ks_field, "melt_rate": melt_rate, "obs_index": obs_index, "obs_value": obs_value, "obs_error": obs_error, "perturbation": perturbation}


def flux_total(padded_head, padded_cond, total_head, conduct, row_global, col_global, total_x, total_y):
    size_x = total_head.shape[1]
    size_y = total_head.shape[2]
    change = jnp.zeros_like(total_head)
    moves = ((-1, 0, row_global > 0), (1, 0, row_global < total_x - 1), (0, -1, col_global > 0), (0, 1, col_global < total_y - 1))
    for shift_x, shift_y, valid in moves:
        near_head = padded_head[:, 1 + shift_x:1 + shift_x + size_x, 1 + shift_y:1 + shift_y + size_y]
        near_cond = padded_cond[:, 1 + shift_x:1 + shift_x + size_x, 1 + shift_y:1 + shift_y + size_y]
        flux = 0.5 * (conduct + near_cond) * (near_head - total_head)
        change = change + jnp.where(valid, flux, jnp.float32(0.0))
    return change

def advance_block(pressure, elevation, ks_field, melt_rate):
    row_global = jnp.arange(NODES_ACROSS, dtype=jnp.int32)[None, :, None]
    col_global = jnp.arange(NODES_DOWNSLOPE, dtype=jnp.int32)[None, None, :]
    for step in range(SUBSTEPS):
        total_head = pressure + elevation[None, :, :]
        conduct = ks_field[None, :, :] * jax.nn.sigmoid(pressure)
        padded_head = jnp.pad(total_head, ((0, 0), (1, 1), (1, 1)))
        padded_cond = jnp.pad(conduct, ((0, 0), (1, 1), (1, 1)))
        change = flux_total(padded_head, padded_cond, total_head, conduct, row_global, col_global, NODES_ACROSS, NODES_DOWNSLOPE)
        pressure = pressure + change + melt_rate
    return pressure

def reference(pressure, elevation, ks_field, melt_rate, obs_index, obs_value, obs_error, perturbation):
    partitioned_domain = pressure.reshape(N_MEM, MEM_DEV, NODES_ACROSS, NODES_DOWNSLOPE)
    snowwater_partitioned = melt_rate.reshape(N_MEM, MEM_DEV, NODES_ACROSS, NODES_DOWNSLOPE)

    def solitary_subdomain(pair):
        return advance_block(pair[0], elevation, ks_field, pair[1])
    predicted_states = lax.map(solitary_subdomain, (partitioned_domain, snowwater_partitioned)).reshape(REPLICA_COUNT, NODES_ACROSS, NODES_DOWNSLOPE)
    raveled_layout = predicted_states.reshape(REPLICA_COUNT, NODES_ACROSS * NODES_DOWNSLOPE)
    observed = jnp.take(raveled_layout, obs_index.astype(jnp.int32), axis=1).T
    scale = obs_error[:, None]
    innovation = (obs_value[:, None] + scale * perturbation - observed) / scale
    anomaly = (observed - jnp.mean(observed, axis=1, keepdims=True)) / scale
    gram = jnp.dot(anomaly.T.astype(jnp.float32), anomaly.astype(jnp.float32), precision=lax.Precision.HIGHEST, preferred_element_type=jnp.float32)
    coupling = jnp.dot(anomaly.T.astype(jnp.float32), innovation.astype(jnp.float32), precision=lax.Precision.HIGHEST, preferred_element_type=jnp.float32)
    system = gram + (REPLICA_COUNT - 1) * jnp.eye(REPLICA_COUNT, dtype=jnp.float32)
    lower = jnp.linalg.cholesky(system)
    weights = jax.scipy.linalg.cho_solve((lower, True), coupling).astype(jnp.bfloat16)
    rounded = raveled_layout.astype(jnp.bfloat16).astype(jnp.float32)
    assimilated_shift = jnp.dot(weights.astype(jnp.float32).T.astype(jnp.float32), rounded.astype(jnp.float32), precision=lax.Precision.HIGHEST, preferred_element_type=jnp.float32)
    return predicted_states + assimilated_shift.reshape(REPLICA_COUNT, NODES_ACROSS, NODES_DOWNSLOPE)
```

```python
import functools

import jax
import jax.numpy as jnp
from jax import lax
from jax.experimental import pallas as pl
from jax.experimental.pallas import tpu as pltpu
from jax.sharding import PartitionSpec as P

SUBSTEPS = 4
HALO = 8
PAD = 2 * HALO
STRIP = 4
CHUNK = 64
F32 = jnp.float32
BF16 = jnp.bfloat16


def kernel(
    n_mem, n_tx, n_ty, share,
    p_hbm, e_hbm, k_hbm, m_hbm, place, packed,
    out,
    p_ext, m_ext, e_ext, k_ext, ping, edges, faces, hot, fore, obs, picks, sums,
    load_sem, row_send, row_recv, edge_send, edge_recv, obs_send, obs_recv,
    fore_send, fore_recv, pick_send, pick_recv, sum_send, sum_recv,
):
    members, size_x, size_y = out.shape
    total = n_mem * members
    n_plane = n_tx * n_ty
    rows = size_x + 2 * PAD
    own = pl.ds(PAD, size_x)
    me_mem = lax.axis_index("mem")
    tx = lax.axis_index("tx")
    ty = lax.axis_index("ty")
    me = tx * n_ty + ty

    def plane(step):
        other = lax.rem(me + step, n_plane)
        return {"tx": other // n_ty, "ty": lax.rem(other, n_ty)}

    def partner(step):
        return {"mem": lax.rem(me_mem + step, n_mem)}

    barrier = pltpu.get_barrier_semaphore()

    def greet(step, carry):
        pl.semaphore_signal(barrier, inc=1, device_id=plane(step))
        return carry

    lax.fori_loop(1, n_plane, greet, 0)
    for step in range(1, n_mem):
        pl.semaphore_signal(barrier, inc=1, device_id=partner(step))

    loads = [
        pltpu.make_async_copy(p_hbm, p_ext.at[:, own, :], load_sem.at[0]),
        pltpu.make_async_copy(m_hbm, m_ext.at[:, own, :], load_sem.at[1]),
        pltpu.make_async_copy(e_hbm, e_ext.at[own, :], load_sem.at[2]),
        pltpu.make_async_copy(k_hbm, k_ext.at[own, :], load_sem.at[3]),
    ]
    for load in loads:
        load.start()
    obs[me] = packed[...]
    pl.semaphore_wait(barrier, n_plane - 1 + n_mem - 1)

    ends = (
        (pl.ds(0, HALO), pl.ds(PAD + size_x, HALO)),
        (pl.ds(size_x - HALO, HALO), pl.ds(HALO, HALO)),
    )

    def row_copies(way):
        source, target = ends[way]
        device = {"tx": tx + (2 * way - 1)}
        pairs = (
            (p_hbm.at[:, source, :], p_ext.at[:, target, :]),
            (m_hbm.at[:, source, :], m_ext.at[:, target, :]),
            (e_hbm.at[source, :], e_ext.at[target, :]),
            (k_hbm.at[source, :], k_ext.at[target, :]),
        )
        return [
            pltpu.make_async_remote_copy(
                src_ref=a, dst_ref=b, send_sem=row_send.at[way, i],
                recv_sem=row_recv.at[way, i], device_id=device,
            )
            for i, (a, b) in enumerate(pairs)
        ]

    send_up, send_down = tx > 0, tx < n_tx - 1
    for way, there in ((0, send_up), (1, send_down)):
        @pl.when(there)
        def _(way=way):
            for copy in row_copies(way):
                copy.start()

    for load in loads:
        load.wait()

    lane = lax.broadcasted_iota(jnp.int32, (1, 128), 1)
    half = 8 * members
    column = lane & 7
    side0 = lane < half
    own_lane = (side0 & (column >= STRIP)) | ((lane >= half) & (column < STRIP))

    def put(base, value, start, source):
        moved = pltpu.roll(value, (start - source) % 128, 1)
        return jnp.where((lane >= start) & (lane < start + STRIP), moved, base)

    def pack(base, first, second, m):
        base = put(base, first[0], 8 * m + STRIP, 0)
        base = put(base, first[1], half + 8 * m, 128 - STRIP)
        base = put(base, second[0], half + 8 * m + STRIP, 0)
        return put(base, second[1], 8 * m, 128 - STRIP)

    def tiles(ref, *at):
        return ref[(*at, own, pl.ds(0, 128))], ref[(*at, own, pl.ds(size_y - 128, 128))]

    base = jnp.zeros((size_x, 128), F32)
    for m in range(members):
        base = pack(base, tiles(p_ext, m), tiles(m_ext, m), m)
    edges[1, 0, own, :] = base
    base = pack(jnp.zeros((size_x, 128), F32), tiles(e_ext), tiles(k_ext), 0)
    width = 8
    while width < half:
        base = base + pltpu.roll(base, width, 1)
        width *= 2
    edges[1, 1, own, :] = base

    spans = {
        -1: (pl.ds(PAD, HALO), pl.ds(PAD + size_x, HALO)),
        0: (own, own),
        1: (pl.ds(PAD + size_x - HALO, HALO), pl.ds(HALO, HALO)),
    }
    around = [(dx, dy) for dx in (-1, 0, 1) for dy in (-1, 0, 1) if (dx, dy) != (0, 0)]

    def inside(dx, dy):
        x, y = tx + dx, ty + dy
        return (x >= 0) & (x < n_tx) & (y >= 0) & (y < n_ty)

    def edge_copy(i):
        dx, dy = around[i]
        source, target = spans[dx]
        return pltpu.make_async_remote_copy(
            src_ref=edges.at[1, :, source, :], dst_ref=edges.at[1 - dy, :, target, :],
            send_sem=edge_send.at[i], recv_sem=edge_recv.at[i],
            device_id={"tx": tx + dx, "ty": ty + dy},
        )

    for i, (dx, dy) in enumerate(around):
        @pl.when(inside(dx, dy))
        def _(i=i):
            edge_copy(i).start()

    def obs_copy(step):
        return pltpu.make_async_remote_copy(
            src_ref=obs.at[me], dst_ref=obs.at[me], send_sem=obs_send.at[step],
            recv_sem=obs_recv.at[step], device_id=plane(step),
        )

    def obs_start(step, carry):
        obs_copy(step).start()
        return carry

    lax.fori_loop(1, n_plane, obs_start, 0)

    n_obs = place.shape[1]
    local_x = place[0:1, :]
    local_y = place[1:2, :]
    hot[...] = jnp.where(
        lax.broadcasted_iota(jnp.int32, (size_y, n_obs), 0) == local_y, F32(1), F32(0)
    ).astype(BF16)

    for way, there, back in ((0, send_up, send_down), (1, send_down, send_up)):
        @pl.when(there)
        def _(way=way):
            for copy in row_copies(way):
                copy.wait_send()

        @pl.when(back)
        def _(way=way):
            for copy in row_copies(way):
                copy.wait_recv()
    for i, (dx, dy) in enumerate(around):
        @pl.when(inside(dx, dy))
        def _(i=i):
            edge_copy(i).wait_send()

        @pl.when(inside(-dx, -dy))
        def _(i=i):
            edge_copy(i).wait_recv()

    k_ext[...] = 0.25 * k_ext[...]

    def unpack(i):
        left, mine, right = edges[0, i], edges[1, i], edges[2, i]
        beside = jnp.where(side0, pltpu.roll(left, half, 1), pltpu.roll(right, half, 1))
        second = jnp.where(own_lane, pltpu.roll(mine, half, 1), jnp.where(side0, left, right))
        return jnp.where(own_lane, mine, beside), second

    pres, melt = unpack(0)
    elev, quarter = unpack(1)
    quarter = 0.25 * quarter
    column_global = ty * size_y + column + jnp.where(side0, -STRIP, size_y - STRIP)
    right_in = (column_global >= 0) & (column_global < n_ty * size_y - 1)

    def down_in(first, count, lanes):
        at = lax.broadcasted_iota(jnp.int32, (count, lanes), 0) + (first - PAD) + tx * size_x
        return (at >= 0) & (at < n_tx * size_x - 1)

    for t in range(SUBSTEPS):
        cond = quarter + quarter * jnp.tanh(0.5 * pres)
        head = pres + elev
        over = jnp.where(
            right_in,
            (cond + pltpu.roll(cond, 127, 1)) * (pltpu.roll(head, 127, 1) - head), F32(0),
        )
        faces[t] = over
        if t < SUBSTEPS - 1:
            down = jnp.where(
                down_in(0, rows, 128),
                (cond + pltpu.roll(cond, rows - 1, 0)) * (pltpu.roll(head, rows - 1, 0) - head),
                F32(0),
            )
            pres = pres + (over - pltpu.roll(over, 1, 1)) + (down - pltpu.roll(down, 1, 0)) + melt

    inner = list(range(PAD, PAD + size_x, CHUNK)) + [PAD + size_x]
    wide = [HALO] + inner[1:-1] + [PAD + size_x + HALO]

    def fore_copy(step, m):
        return pltpu.make_async_remote_copy(
            src_ref=fore.at[me_mem, m], dst_ref=fore.at[me_mem, m],
            send_sem=fore_send.at[step, m], recv_sem=fore_recv.at[step, m],
            device_id=partner(step),
        )

    def member(m, carry):
        for t in range(SUBSTEPS):
            cuts = wide if t < SUBSTEPS - 1 else inner
            for a, b in zip(cuts[:-1], cuts[1:]):
                count = b - a + 2 * HALO
                span = pl.ds(a - HALO, count)
                p = p_ext[m, span, :] if t == 0 else ping[(t - 1) % 2, span, :]
                k = k_ext[span, :]
                cond = k + k * jnp.tanh(0.5 * p)
                head = p + e_ext[span, :]
                down = (cond + pltpu.roll(cond, count - 1, 0)) * (
                    pltpu.roll(head, count - 1, 0) - head
                )
                if a <= PAD or b >= PAD + size_x:
                    down = jnp.where(down_in(a - HALO, count, size_y), down, F32(0))
                upright = (down - pltpu.roll(down, 1, 0))[HALO : count - HALO]
                c, h = cond[HALO : count - HALO], head[HALO : count - HALO]
                over = (c + pltpu.roll(c, size_y - 1, 1)) * (pltpu.roll(h, size_y - 1, 1) - h)
                face = faces[t, pl.ds(a, b - a), :]
                low = pltpu.roll(face, 128 - (STRIP - 1) - 8 * m, 1)
                high = pltpu.roll(face, 128 - half - STRIP - 8 * m, 1)
                over = jnp.concatenate(
                    [over[:, :-128], jnp.where(lane == 127, high, over[:, -128:])], axis=1
                )
                back = pltpu.roll(over, 1, 1)
                back = jnp.concatenate(
                    [jnp.where(lane == 0, low, back[:, :128]), back[:, 128:]], axis=1
                )
                new = (
                    p[HALO : count - HALO] + (over - back) + upright
                    + m_ext[m, pl.ds(a, b - a), :]
                )
                if t < SUBSTEPS - 1:
                    ping[t % 2, pl.ds(a, b - a), :] = new
                else:
                    out[m, pl.ds(a - PAD, b - a), :] = new
                    fore[me_mem, m, pl.ds(a - PAD, b - a), :] = new.astype(BF16)
        for step in range(1, n_mem):
            fore_copy(step, m).start()
        value = out[m]
        top = value.astype(BF16)
        rest = (value - top.astype(F32)).astype(BF16)
        piece = 256 if n_obs % 256 == 0 else n_obs
        row = lax.broadcasted_iota(jnp.int32, (size_x, piece), 0)
        for at in range(0, n_obs, piece):
            some = hot[:, at : at + piece]
            got = jnp.dot(top, some, preferred_element_type=F32) + jnp.dot(
                rest, some, preferred_element_type=F32
            )
            got = jnp.where(row == local_x[:, at : at + piece], got, F32(0))
            picks[pl.ds(me_mem * members + m, 1), at : at + piece] = jnp.sum(
                got, axis=0, keepdims=True
            )
        return carry

    lax.fori_loop(0, members, member, 0)

    mine = pl.ds(pl.multiple_of(me_mem * members, 8), members)

    def pick_copy(step):
        return pltpu.make_async_remote_copy(
            src_ref=picks.at[mine, :], dst_ref=picks.at[mine, :],
            send_sem=pick_send.at[step], recv_sem=pick_recv.at[step], device_id=partner(step),
        )

    for step in range(1, n_mem):
        pick_copy(step).start()

    def obs_wait(step, carry):
        obs_copy(step).wait()
        return carry

    lax.fori_loop(1, n_plane, obs_wait, 0)
    per = 128 // share
    parts = []
    for first in range(0, n_plane, per):
        part = obs[first]
        for j in range(1, per):
            part = part + pltpu.roll(obs[first + j], j * share, 1)
        parts.append(part)
    every = jnp.concatenate(parts, axis=1)
    noise, value, error = every[:members], every[members : members + 1], every[members + 1 : members + 2]
    here = (local_x >= 0) & (local_x < size_x) & (local_y >= 0) & (local_y < size_y)

    for step in range(1, n_mem):
        pick_copy(step).wait()
    innovation = (value + error * noise - picks[mine, :]) / error
    seen = picks[...]
    anomaly = (seen - jnp.mean(seen, axis=0, keepdims=True)) / error
    anomaly = jnp.where(here, anomaly, F32(0))
    lanes = sums.shape[2]
    both = jnp.concatenate(
        [anomaly, innovation, jnp.zeros((lanes - total - members, n_obs), F32)], axis=0
    )
    sums[me] = lax.dot_general(
        anomaly, both, (((1,), (1,)), ((), ())),
        precision=lax.Precision.HIGHEST, preferred_element_type=F32,
    )

    def sum_copy(step):
        return pltpu.make_async_remote_copy(
            src_ref=sums.at[me], dst_ref=sums.at[me], send_sem=sum_send.at[step],
            recv_sem=sum_recv.at[step], device_id=plane(step),
        )

    def sum_start(step, carry):
        sum_copy(step).start()
        return carry

    def sum_wait(step, carry):
        sum_copy(step).wait()
        return carry

    lax.fori_loop(1, n_plane, sum_start, 0)
    lax.fori_loop(1, n_plane, sum_wait, 0)
    ri = lax.broadcasted_iota(jnp.int32, (total, lanes), 0)
    ci = lax.broadcasted_iota(jnp.int32, (total, lanes), 1)
    system = jnp.sum(sums[...], axis=0) + jnp.where(ri == ci, F32(total - 1), F32(0))
    for k in range(total):
        pivot = system[k : k + 1, :] / system[k : k + 1, k : k + 1]
        system = jnp.where(ri == k, pivot, system - system[:, k : k + 1] * pivot)
    weights = system.astype(BF16)

    group = 16
    ra = lax.broadcasted_iota(jnp.int32, (members * group, lanes), 0)
    rb = lax.broadcasted_iota(jnp.int32, (members * group, lanes), 1)
    choose = jnp.where(rb - total == ra // group, F32(1), F32(0)).astype(BF16)
    spread = lax.dot_general(
        choose, weights, (((1,), (1,)), ((), ())), preferred_element_type=F32
    ).astype(BF16)
    ca = lax.broadcasted_iota(jnp.int32, (total, total * group), 0)
    cb = lax.broadcasted_iota(jnp.int32, (total, total * group), 1)
    repeat = jnp.where(cb // group == ca, F32(1), F32(0)).astype(BF16)
    spread = jnp.dot(spread, repeat, preferred_element_type=F32)
    da = lax.broadcasted_iota(jnp.int32, spread.shape, 0)
    db = lax.broadcasted_iota(jnp.int32, spread.shape, 1)
    spread = jnp.where((da & (group - 1)) == (db & (group - 1)), spread, F32(0)).astype(BF16)

    def fore_wait(m, carry):
        for step in range(1, n_mem):
            fore_copy(step, m).wait()
        return carry

    lax.fori_loop(0, members, fore_wait, 0)

    def finish(g, carry):
        span = pl.ds(pl.multiple_of(g * group, group), group)
        block = fore[:, :, span, :].reshape(total * group, size_y)
        shift = jnp.dot(spread, block, preferred_element_type=F32)
        out[:, span, :] = out[:, span, :] + shift.reshape(members, group, size_y)
        return carry

    lax.fori_loop(0, size_x // group, finish, 0)


def local(pressure, elevation, ks_field, melt_rate, obs_index, obs_value, obs_error, perturbation):
    members, size_x, size_y = pressure.shape
    n_mem, n_tx, n_ty = (lax.axis_size(a) for a in ("mem", "tx", "ty"))
    n_plane = n_tx * n_ty
    total = n_mem * members
    share = obs_value.shape[0]
    n_obs = obs_index.shape[0]
    total_y = size_y * n_ty
    place = jnp.stack(
        [
            obs_index // total_y - lax.axis_index("tx") * size_x,
            obs_index % total_y - lax.axis_index("ty") * size_y,
        ]
    )
    packed = jnp.concatenate([perturbation.T, obs_value[None], obs_error[None]], axis=0)
    height = -(-(members + 2) // 8) * 8
    packed = jnp.pad(packed, ((0, height - members - 2), (0, 128 - share)))
    lanes = -(-(total + members) // 128) * 128
    rows = size_x + 2 * PAD
    dma = pltpu.SemaphoreType.DMA
    vmem = pl.BlockSpec(memory_space=pltpu.VMEM)
    hbm = pl.BlockSpec(memory_space=pl.ANY)
    return pl.pallas_call(
        functools.partial(kernel, n_mem, n_tx, n_ty, share),
        out_shape=jax.ShapeDtypeStruct(pressure.shape, F32),
        in_specs=[hbm] * 4 + [vmem] * 2,
        out_specs=vmem,
        scratch_shapes=[
            pltpu.VMEM((members, rows, size_y), F32),
            pltpu.VMEM((members, rows, size_y), F32),
            pltpu.VMEM((rows, size_y), F32),
            pltpu.VMEM((rows, size_y), F32),
            pltpu.VMEM((2, rows, size_y), F32),
            pltpu.VMEM((3, 2, rows, 128), F32),
            pltpu.VMEM((SUBSTEPS, rows, 128), F32),
            pltpu.VMEM((size_y, n_obs), BF16),
            pltpu.VMEM((n_mem, members, size_x, size_y), BF16),
            pltpu.VMEM((n_plane, height, 128), F32),
            pltpu.VMEM((total, n_obs), F32),
            pltpu.VMEM((n_plane, total, lanes), F32),
            dma((4,)), dma((2, 4)), dma((2, 4)), dma((8,)), dma((8,)),
            dma((n_plane,)), dma((n_plane,)),
            dma((n_mem, members)), dma((n_mem, members)),
            dma((n_mem,)), dma((n_mem,)), dma((n_plane,)), dma((n_plane,)),
        ],
        compiler_params=pltpu.CompilerParams(
            collective_id=0, has_side_effects=True, vmem_limit_bytes=48 * 2**20
        ),
    )(pressure, elevation, ks_field, melt_rate, place, packed)


def solution(mesh):
    placed = (
        P("mem", "tx", "ty"),
        P("tx", "ty"),
        P("tx", "ty"),
        P("mem", "tx", "ty"),
        P(),
        P(("tx", "ty")),
        P(("tx", "ty")),
        P(("tx", "ty"), "mem"),
    )
    return jax.shard_map(
        local, mesh=mesh, in_specs=placed, out_specs=P("mem", "tx", "ty"), check_vma=False
    )
```

```python
import functools

import jax
import jax.numpy as jnp
from jax import lax
from jax.experimental import pallas as pl
from jax.experimental.pallas import tpu as pltpu
from jax.sharding import PartitionSpec as P

SUBSTEPS = 4
HALO = 8
PAD = 2 * HALO
STRIP = 4
CHUNK = 64
LATE = 2
F32 = jnp.float32
BF16 = jnp.bfloat16


def kernel(
    n_mem, n_tx, n_ty, share,
    p_hbm, e_hbm, k_hbm, m_hbm, index_hbm, value_hbm, error_hbm, noise_hbm,
    out,
    p_ext, m_ext, e_ext, k_ext, ping, edges, faces, hot, fore, obs, picks, sums,
    index, own_value, own_error, own_noise,
    load_sem, row_send, row_recv, edge_send, edge_recv, obs_send, obs_recv,
    fore_send, fore_recv, pick_send, pick_recv, sum_send, sum_recv,
):
    members, size_x, size_y = out.shape
    total = n_mem * members
    n_plane = n_tx * n_ty
    rows = size_x + 2 * PAD
    own = pl.ds(PAD, size_x)
    me_mem = lax.axis_index("mem")
    tx = lax.axis_index("tx")
    ty = lax.axis_index("ty")
    me = tx * n_ty + ty

    def plane(step):
        other = lax.rem(me + step, n_plane)
        return {"tx": other // n_ty, "ty": lax.rem(other, n_ty)}

    def partner(step):
        return {"mem": lax.rem(me_mem + step, n_mem)}

    barrier = pltpu.get_barrier_semaphore()

    def greet(step, carry):
        pl.semaphore_signal(barrier, inc=1, device_id=plane(step))
        return carry

    lax.fori_loop(1, n_plane, greet, 0)
    for step in range(1, n_mem):
        pl.semaphore_signal(barrier, inc=1, device_id=partner(step))

    loads = [
        pltpu.make_async_copy(p_hbm, p_ext.at[:, own, :], load_sem.at[0]),
        pltpu.make_async_copy(m_hbm, m_ext.at[:, own, :], load_sem.at[1]),
        pltpu.make_async_copy(e_hbm, e_ext.at[own, :], load_sem.at[2]),
        pltpu.make_async_copy(k_hbm, k_ext.at[own, :], load_sem.at[3]),
    ]
    small = [
        pltpu.make_async_copy(index_hbm, index, load_sem.at[4]),
        pltpu.make_async_copy(value_hbm, own_value, load_sem.at[5]),
        pltpu.make_async_copy(error_hbm, own_error, load_sem.at[6]),
        pltpu.make_async_copy(noise_hbm, own_noise, load_sem.at[7]),
    ]
    for load in loads + small:
        load.start()
    obs[me] = jnp.zeros(obs.shape[1:], F32)
    pl.semaphore_wait(barrier, n_plane - 1 + n_mem - 1)

    ends = (
        (pl.ds(0, HALO), pl.ds(PAD + size_x, HALO)),
        (pl.ds(size_x - HALO, HALO), pl.ds(HALO, HALO)),
    )

    def row_copies(way):
        source, target = ends[way]
        device = {"tx": tx + (2 * way - 1)}
        pairs = (
            (p_hbm.at[:, source, :], p_ext.at[:, target, :]),
            (m_hbm.at[:, source, :], m_ext.at[:, target, :]),
            (e_hbm.at[source, :], e_ext.at[target, :]),
            (k_hbm.at[source, :], k_ext.at[target, :]),
        )
        return [
            pltpu.make_async_remote_copy(
                src_ref=a, dst_ref=b, send_sem=row_send.at[way, i],
                recv_sem=row_recv.at[way, i], device_id=device,
            )
            for i, (a, b) in enumerate(pairs)
        ]

    send_up, send_down = tx > 0, tx < n_tx - 1
    for way, there in ((0, send_up), (1, send_down)):
        @pl.when(there)
        def _(way=way):
            for copy in row_copies(way):
                copy.start()

    for load in loads:
        load.wait()

    lane = lax.broadcasted_iota(jnp.int32, (1, 128), 1)
    half = 8 * members
    column = lane & 7
    side0 = lane < half
    own_lane = (side0 & (column >= STRIP)) | ((lane >= half) & (column < STRIP))

    def put(base, value, start, source):
        moved = pltpu.roll(value, (start - source) % 128, 1)
        return jnp.where((lane >= start) & (lane < start + STRIP), moved, base)

    def pack(base, first, second, m):
        base = put(base, first[0], 8 * m + STRIP, 0)
        base = put(base, first[1], half + 8 * m, 128 - STRIP)
        base = put(base, second[0], half + 8 * m + STRIP, 0)
        return put(base, second[1], 8 * m, 128 - STRIP)

    def tiles(ref, *at):
        return ref[(*at, own, pl.ds(0, 128))], ref[(*at, own, pl.ds(size_y - 128, 128))]

    base = jnp.zeros((size_x, 128), F32)
    for m in range(members):
        base = pack(base, tiles(p_ext, m), tiles(m_ext, m), m)
    edges[1, 0, own, :] = base
    base = pack(jnp.zeros((size_x, 128), F32), tiles(e_ext), tiles(k_ext), 0)
    width = 8
    while width < half:
        base = base + pltpu.roll(base, width, 1)
        width *= 2
    edges[1, 1, own, :] = base

    spans = {
        -1: (pl.ds(PAD, HALO), pl.ds(PAD + size_x, HALO)),
        0: (own, own),
        1: (pl.ds(PAD + size_x - HALO, HALO), pl.ds(HALO, HALO)),
    }
    around = [(dx, dy) for dx in (-1, 0, 1) for dy in (-1, 0, 1) if (dx, dy) != (0, 0)]

    def inside(dx, dy):
        x, y = tx + dx, ty + dy
        return (x >= 0) & (x < n_tx) & (y >= 0) & (y < n_ty)

    def edge_copy(i):
        dx, dy = around[i]
        source, target = spans[dx]
        return pltpu.make_async_remote_copy(
            src_ref=edges.at[1, :, source, :], dst_ref=edges.at[1 - dy, :, target, :],
            send_sem=edge_send.at[i], recv_sem=edge_recv.at[i],
            device_id={"tx": tx + dx, "ty": ty + dy},
        )

    for i, (dx, dy) in enumerate(around):
        @pl.when(inside(dx, dy))
        def _(i=i):
            edge_copy(i).start()

    def obs_copy(step):
        return pltpu.make_async_remote_copy(
            src_ref=obs.at[me], dst_ref=obs.at[me], send_sem=obs_send.at[step],
            recv_sem=obs_recv.at[step], device_id=plane(step),
        )

    def obs_start(step, carry):
        obs_copy(step).start()
        return carry

    for load in small:
        load.wait()
    obs[me, :members, :share] = own_noise[...]
    obs[me, members : members + 1, :share] = own_value[...]
    obs[me, members + 1 : members + 2, :share] = own_error[...]
    lax.fori_loop(1, n_plane, obs_start, 0)

    n_obs = index.shape[1]
    total_y = n_ty * size_y
    if total_y & (total_y - 1):
        global_x = index[...] // total_y
    else:
        global_x = lax.shift_right_logical(index[...], total_y.bit_length() - 1)
    local_x = global_x - tx * size_x
    local_y = index[...] - global_x * total_y - ty * size_y
    hot[...] = jnp.where(
        lax.broadcasted_iota(jnp.int32, (size_y, n_obs), 0) == local_y, F32(1), F32(0)
    ).astype(BF16)

    for way, there, back in ((0, send_up, send_down), (1, send_down, send_up)):
        @pl.when(there)
        def _(way=way):
            for copy in row_copies(way):
                copy.wait_send()

        @pl.when(back)
        def _(way=way):
            for copy in row_copies(way):
                copy.wait_recv()
    for i, (dx, dy) in enumerate(around):
        @pl.when(inside(dx, dy))
        def _(i=i):
            edge_copy(i).wait_send()

        @pl.when(inside(-dx, -dy))
        def _(i=i):
            edge_copy(i).wait_recv()

    k_ext[...] = 0.25 * k_ext[...]

    def unpack(i):
        left, mine, right = edges[0, i], edges[1, i], edges[2, i]
        beside = jnp.where(side0, pltpu.roll(left, half, 1), pltpu.roll(right, half, 1))
        second = jnp.where(own_lane, pltpu.roll(mine, half, 1), jnp.where(side0, left, right))
        return jnp.where(own_lane, mine, beside), second

    pres, melt = unpack(0)
    elev, quarter = unpack(1)
    quarter = 0.25 * quarter
    column_global = ty * size_y + column + jnp.where(side0, -STRIP, size_y - STRIP)
    right_in = (column_global >= 0) & (column_global < n_ty * size_y - 1)

    def down_in(first, count, lanes):
        at = lax.broadcasted_iota(jnp.int32, (count, lanes), 0) + (first - PAD) + tx * size_x
        return (at >= 0) & (at < n_tx * size_x - 1)

    for t in range(SUBSTEPS):
        cond = quarter + quarter * jnp.tanh(0.5 * pres)
        head = pres + elev
        over = jnp.where(
            right_in,
            (cond + pltpu.roll(cond, 127, 1)) * (pltpu.roll(head, 127, 1) - head), F32(0),
        )
        faces[t] = over
        if t < SUBSTEPS - 1:
            down = jnp.where(
                down_in(0, rows, 128),
                (cond + pltpu.roll(cond, rows - 1, 0)) * (pltpu.roll(head, rows - 1, 0) - head),
                F32(0),
            )
            pres = pres + (over - pltpu.roll(over, 1, 1)) + (down - pltpu.roll(down, 1, 0)) + melt

    inner = list(range(PAD, PAD + size_x, CHUNK)) + [PAD + size_x]
    wide = [HALO] + inner[1:-1] + [PAD + size_x + HALO]

    def fore_copy(step, m):
        return pltpu.make_async_remote_copy(
            src_ref=fore.at[me_mem, m], dst_ref=fore.at[me_mem, m],
            send_sem=fore_send.at[step, m], recv_sem=fore_recv.at[step, m],
            device_id=partner(step),
        )

    def member(m, carry):
        for t in range(SUBSTEPS):
            cuts = wide if t < SUBSTEPS - 1 else inner
            for a, b in zip(cuts[:-1], cuts[1:]):
                count = b - a + 2 * HALO
                span = pl.ds(a - HALO, count)
                p = p_ext[m, span, :] if t == 0 else ping[(t - 1) % 2, span, :]
                k = k_ext[span, :]
                cond = k + k * jnp.tanh(0.5 * p)
                head = p + e_ext[span, :]
                down = (cond + pltpu.roll(cond, count - 1, 0)) * (
                    pltpu.roll(head, count - 1, 0) - head
                )
                if a <= PAD or b >= PAD + size_x:
                    down = jnp.where(down_in(a - HALO, count, size_y), down, F32(0))
                upright = (down - pltpu.roll(down, 1, 0))[HALO : count - HALO]
                c, h = cond[HALO : count - HALO], head[HALO : count - HALO]
                over = (c + pltpu.roll(c, size_y - 1, 1)) * (pltpu.roll(h, size_y - 1, 1) - h)
                face = faces[t, pl.ds(a, b - a), :]
                low = pltpu.roll(face, 128 - (STRIP - 1) - 8 * m, 1)
                high = pltpu.roll(face, 128 - half - STRIP - 8 * m, 1)
                over = jnp.concatenate(
                    [over[:, :-128], jnp.where(lane == 127, high, over[:, -128:])], axis=1
                )
                back = pltpu.roll(over, 1, 1)
                back = jnp.concatenate(
                    [jnp.where(lane == 0, low, back[:, :128]), back[:, 128:]], axis=1
                )
                new = (
                    p[HALO : count - HALO] + (over - back) + upright
                    + m_ext[m, pl.ds(a, b - a), :]
                )
                if t < SUBSTEPS - 1:
                    ping[t % 2, pl.ds(a, b - a), :] = new
                else:
                    out[m, pl.ds(a - PAD, b - a), :] = new
                    fore[me_mem, m, pl.ds(a - PAD, b - a), :] = new.astype(BF16)
        @pl.when(m < members - LATE)
        def _():
            for step in range(1, n_mem):
                fore_copy(step, m).start()

        value = out[m]
        top = value.astype(BF16)
        rest = (value - top.astype(F32)).astype(BF16)
        piece = 256 if n_obs % 256 == 0 else n_obs
        row = lax.broadcasted_iota(jnp.int32, (size_x, piece), 0)
        for at in range(0, n_obs, piece):
            some = hot[:, at : at + piece]
            got = jnp.dot(top, some, preferred_element_type=F32) + jnp.dot(
                rest, some, preferred_element_type=F32
            )
            got = jnp.where(row == local_x[:, at : at + piece], got, F32(0))
            picks[pl.ds(me_mem * members + m, 1), at : at + piece] = jnp.sum(
                got, axis=0, keepdims=True
            )
        return carry

    lax.fori_loop(0, members, member, 0)

    mine = pl.ds(pl.multiple_of(me_mem * members, 8), members)

    def pick_copy(step):
        return pltpu.make_async_remote_copy(
            src_ref=picks.at[mine, :], dst_ref=picks.at[mine, :],
            send_sem=pick_send.at[step], recv_sem=pick_recv.at[step], device_id=partner(step),
        )

    for step in range(1, n_mem):
        pick_copy(step).start()
    for m in range(members - LATE, members):
        for step in range(1, n_mem):
            fore_copy(step, m).start()

    def obs_wait(step, carry):
        obs_copy(step).wait()
        return carry

    lax.fori_loop(1, n_plane, obs_wait, 0)
    per = 128 // share
    parts = []
    for first in range(0, n_plane, per):
        part = obs[first]
        for j in range(1, per):
            part = part + pltpu.roll(obs[first + j], j * share, 1)
        parts.append(part)
    every = jnp.concatenate(parts, axis=1)
    noise, value, error = every[:members], every[members : members + 1], every[members + 1 : members + 2]
    here = (local_x >= 0) & (local_x < size_x) & (local_y >= 0) & (local_y < size_y)

    for step in range(1, n_mem):
        pick_copy(step).wait()
    innovation = (value + error * noise - picks[mine, :]) / error
    seen = picks[...]
    anomaly = (seen - jnp.mean(seen, axis=0, keepdims=True)) / error
    anomaly = jnp.where(here, anomaly, F32(0))
    lanes = sums.shape[2]
    both = jnp.concatenate(
        [anomaly, innovation, jnp.zeros((lanes - total - members, n_obs), F32)], axis=0
    )
    sums[me] = lax.dot_general(
        anomaly, both, (((1,), (1,)), ((), ())),
        precision=lax.Precision.HIGHEST, preferred_element_type=F32,
    )

    def sum_copy(step):
        return pltpu.make_async_remote_copy(
            src_ref=sums.at[me], dst_ref=sums.at[me], send_sem=sum_send.at[step],
            recv_sem=sum_recv.at[step], device_id=plane(step),
        )

    def sum_start(step, carry):
        sum_copy(step).start()
        return carry

    def sum_wait(step, carry):
        sum_copy(step).wait()
        return carry

    lax.fori_loop(1, n_plane, sum_start, 0)
    lax.fori_loop(1, n_plane, sum_wait, 0)
    ri = lax.broadcasted_iota(jnp.int32, (total, lanes), 0)
    ci = lax.broadcasted_iota(jnp.int32, (total, lanes), 1)
    system = jnp.sum(sums[...], axis=0) + jnp.where(ri == ci, F32(total - 1), F32(0))
    for k in range(total):
        pivot = system[k : k + 1, :] / system[k : k + 1, k : k + 1]
        system = jnp.where(ri == k, pivot, system - system[:, k : k + 1] * pivot)
    weights = system.astype(BF16)

    group = 16
    ra = lax.broadcasted_iota(jnp.int32, (members * group, lanes), 0)
    rb = lax.broadcasted_iota(jnp.int32, (members * group, lanes), 1)
    choose = jnp.where(rb - total == ra // group, F32(1), F32(0)).astype(BF16)
    spread = lax.dot_general(
        choose, weights, (((1,), (1,)), ((), ())), preferred_element_type=F32
    ).astype(BF16)
    ca = lax.broadcasted_iota(jnp.int32, (total, total * group), 0)
    cb = lax.broadcasted_iota(jnp.int32, (total, total * group), 1)
    repeat = jnp.where(cb // group == ca, F32(1), F32(0)).astype(BF16)
    spread = jnp.dot(spread, repeat, preferred_element_type=F32)
    da = lax.broadcasted_iota(jnp.int32, spread.shape, 0)
    db = lax.broadcasted_iota(jnp.int32, spread.shape, 1)
    spread = jnp.where((da & (group - 1)) == (db & (group - 1)), spread, F32(0)).astype(BF16)

    def fore_wait(m, carry):
        for step in range(1, n_mem):
            fore_copy(step, m).wait()
        return carry

    lax.fori_loop(0, members, fore_wait, 0)

    def finish(g, carry):
        span = pl.ds(pl.multiple_of(g * group, group), group)
        block = fore[:, :, span, :].reshape(total * group, size_y)
        shift = jnp.dot(spread, block, preferred_element_type=F32)
        out[:, span, :] = out[:, span, :] + shift.reshape(members, group, size_y)
        return carry

    lax.fori_loop(0, size_x // group, finish, 0)


def local(pressure, elevation, ks_field, melt_rate, obs_index, obs_value, obs_error, perturbation):
    members, size_x, size_y = pressure.shape
    n_mem, n_tx, n_ty = (lax.axis_size(a) for a in ("mem", "tx", "ty"))
    n_plane = n_tx * n_ty
    total = n_mem * members
    share = obs_value.shape[0]
    n_obs = obs_index.shape[0]
    height = -(-(members + 2) // 8) * 8
    lanes = -(-(total + members) // 128) * 128
    rows = size_x + 2 * PAD
    dma = pltpu.SemaphoreType.DMA
    vmem = pl.BlockSpec(memory_space=pltpu.VMEM)
    hbm = pl.BlockSpec(memory_space=pltpu.HBM)
    return pl.pallas_call(
        functools.partial(kernel, n_mem, n_tx, n_ty, share),
        out_shape=jax.ShapeDtypeStruct(pressure.shape, F32),
        in_specs=[hbm] * 8,
        out_specs=vmem,
        scratch_shapes=[
            pltpu.VMEM((members, rows, size_y), F32),
            pltpu.VMEM((members, rows, size_y), F32),
            pltpu.VMEM((rows, size_y), F32),
            pltpu.VMEM((rows, size_y), F32),
            pltpu.VMEM((2, rows, size_y), F32),
            pltpu.VMEM((3, 2, rows, 128), F32),
            pltpu.VMEM((SUBSTEPS, rows, 128), F32),
            pltpu.VMEM((size_y, n_obs), BF16),
            pltpu.VMEM((n_mem, members, size_x, size_y), BF16),
            pltpu.VMEM((n_plane, height, 128), F32),
            pltpu.VMEM((total, n_obs), F32),
            pltpu.VMEM((n_plane, total, lanes), F32),
            pltpu.VMEM((1, n_obs), jnp.int32),
            pltpu.VMEM((1, share), F32),
            pltpu.VMEM((1, share), F32),
            pltpu.VMEM((members, share), F32),
            dma((8,)), dma((2, 4)), dma((2, 4)), dma((8,)), dma((8,)),
            dma((n_plane,)), dma((n_plane,)),
            dma((n_mem, members)), dma((n_mem, members)),
            dma((n_mem,)), dma((n_mem,)), dma((n_plane,)), dma((n_plane,)),
        ],
        compiler_params=pltpu.CompilerParams(
            collective_id=0, has_side_effects=True, vmem_limit_bytes=57 * 2**20
        ),
    )(
        pressure, elevation, ks_field, melt_rate,
        obs_index[None], obs_value[None], obs_error[None], perturbation.T,
    )


def solution(mesh):
    placed = (
        P("mem", "tx", "ty"),
        P("tx", "ty"),
        P("tx", "ty"),
        P("mem", "tx", "ty"),
        P(),
        P(("tx", "ty")),
        P(("tx", "ty")),
        P(("tx", "ty"), "mem"),
    )
    return jax.shard_map(
        local, mesh=mesh, in_specs=placed, out_specs=P("mem", "tx", "ty"), check_vma=False
    )
```

```python
import functools

import jax
import jax.numpy as jnp
from jax import lax
from jax.experimental import pallas as pl
from jax.experimental.pallas import tpu as pltpu
from jax.sharding import PartitionSpec as P

SUBSTEPS = 4
HALO = 8
PAD = 2 * HALO
STRIP = 4
CHUNK = 64
SLABS = 4
LATE = 3
F32 = jnp.float32
BF16 = jnp.bfloat16


def kernel(
    n_mem, n_tx, n_ty, share,
    p_hbm, e_hbm, k_hbm, m_hbm, index_hbm, value_hbm, error_hbm, noise_hbm,
    out_hbm,
    out, p_ext, m_ext, e_ext, k_ext, ping, edges, faces, hot, fore, obs, picks, sums,
    index, own_value, own_error, own_noise,
    load_sem, row_send, row_recv, edge_send, edge_recv, obs_send, obs_recv,
    fore_send, fore_recv, late_send, late_recv, pick_send, pick_recv, sum_send, sum_recv,
):
    members, size_x, size_y = out.shape
    total = n_mem * members
    n_plane = n_tx * n_ty
    rows = size_x + 2 * PAD
    own = pl.ds(PAD, size_x)
    me_mem = lax.axis_index("mem")
    tx = lax.axis_index("tx")
    ty = lax.axis_index("ty")
    me = tx * n_ty + ty

    def plane(step):
        other = lax.rem(me + step, n_plane)
        return {"tx": other // n_ty, "ty": lax.rem(other, n_ty)}

    def partner(step):
        return {"mem": lax.rem(me_mem + step, n_mem)}

    barrier = pltpu.get_barrier_semaphore()

    def greet(step, carry):
        pl.semaphore_signal(barrier, inc=1, device_id=plane(step))
        return carry

    for step in range(1, n_plane):
        greet(step, 0)
    for step in range(1, n_mem):
        pl.semaphore_signal(barrier, inc=1, device_id=partner(step))

    loads = [
        pltpu.make_async_copy(p_hbm, p_ext.at[:, own, :], load_sem.at[0]),
        pltpu.make_async_copy(m_hbm, m_ext.at[:, own, :], load_sem.at[1]),
        pltpu.make_async_copy(e_hbm, e_ext.at[own, :], load_sem.at[2]),
        pltpu.make_async_copy(k_hbm, k_ext.at[own, :], load_sem.at[3]),
    ]
    small = [
        pltpu.make_async_copy(index_hbm, index, load_sem.at[4]),
        pltpu.make_async_copy(value_hbm, own_value, load_sem.at[5]),
        pltpu.make_async_copy(error_hbm, own_error, load_sem.at[6]),
        pltpu.make_async_copy(noise_hbm, own_noise, load_sem.at[7]),
    ]
    for load in loads + small:
        load.start()
    obs[me] = jnp.zeros(obs.shape[1:], F32)
    pl.semaphore_wait(barrier, n_plane - 1 + n_mem - 1)

    ends = (
        (pl.ds(0, HALO), pl.ds(PAD + size_x, HALO)),
        (pl.ds(size_x - HALO, HALO), pl.ds(HALO, HALO)),
    )

    def row_copies(way):
        source, target = ends[way]
        device = {"tx": tx + (2 * way - 1)}
        pairs = (
            (p_hbm.at[:, source, :], p_ext.at[:, target, :]),
            (m_hbm.at[:, source, :], m_ext.at[:, target, :]),
            (e_hbm.at[source, :], e_ext.at[target, :]),
            (k_hbm.at[source, :], k_ext.at[target, :]),
        )
        return [
            pltpu.make_async_remote_copy(
                src_ref=a, dst_ref=b, send_sem=row_send.at[way, i],
                recv_sem=row_recv.at[way, i], device_id=device,
            )
            for i, (a, b) in enumerate(pairs)
        ]

    send_up, send_down = tx > 0, tx < n_tx - 1
    for way, there in ((0, send_up), (1, send_down)):
        @pl.when(there)
        def _(way=way):
            for copy in row_copies(way):
                copy.start()

    for load in loads:
        load.wait()

    lane = lax.broadcasted_iota(jnp.int32, (1, 128), 1)
    half = 8 * members
    column = lane & 7
    side0 = lane < half
    own_lane = (side0 & (column >= STRIP)) | ((lane >= half) & (column < STRIP))

    def put(base, value, start, source):
        moved = pltpu.roll(value, (start - source) % 128, 1)
        return jnp.where((lane >= start) & (lane < start + STRIP), moved, base)

    def pack(base, first, second, m):
        base = put(base, first[0], 8 * m + STRIP, 0)
        base = put(base, first[1], half + 8 * m, 128 - STRIP)
        base = put(base, second[0], half + 8 * m + STRIP, 0)
        return put(base, second[1], 8 * m, 128 - STRIP)

    def tiles(ref, *at):
        return ref[(*at, own, pl.ds(0, 128))], ref[(*at, own, pl.ds(size_y - 128, 128))]

    base = jnp.zeros((size_x, 128), F32)
    for m in range(members):
        base = pack(base, tiles(p_ext, m), tiles(m_ext, m), m)
    edges[1, 0, own, :] = base
    base = pack(jnp.zeros((size_x, 128), F32), tiles(e_ext), tiles(k_ext), 0)
    width = 8
    while width < half:
        base = base + pltpu.roll(base, width, 1)
        width *= 2
    edges[1, 1, own, :] = base

    spans = {
        -1: (pl.ds(PAD, HALO), pl.ds(PAD + size_x, HALO)),
        0: (own, own),
        1: (pl.ds(PAD + size_x - HALO, HALO), pl.ds(HALO, HALO)),
    }
    around = [(dx, dy) for dx in (-1, 0, 1) for dy in (-1, 0, 1) if (dx, dy) != (0, 0)]

    def inside(dx, dy):
        x, y = tx + dx, ty + dy
        return (x >= 0) & (x < n_tx) & (y >= 0) & (y < n_ty)

    def edge_copy(i):
        dx, dy = around[i]
        source, target = spans[dx]
        return pltpu.make_async_remote_copy(
            src_ref=edges.at[1, :, source, :], dst_ref=edges.at[1 - dy, :, target, :],
            send_sem=edge_send.at[i], recv_sem=edge_recv.at[i],
            device_id={"tx": tx + dx, "ty": ty + dy},
        )

    for i, (dx, dy) in enumerate(around):
        @pl.when(inside(dx, dy))
        def _(i=i):
            edge_copy(i).start()

    def obs_copy(step):
        return pltpu.make_async_remote_copy(
            src_ref=obs.at[me], dst_ref=obs.at[me], send_sem=obs_send.at[step],
            recv_sem=obs_recv.at[step], device_id=plane(step),
        )

    def obs_start(step, carry):
        obs_copy(step).start()
        return carry

    for load in small:
        load.wait()
    obs[me, :members, :share] = own_noise[...]
    obs[me, members : members + 1, :share] = own_value[...]
    obs[me, members + 1 : members + 2, :share] = own_error[...]
    lax.fori_loop(1, n_plane, obs_start, 0)

    n_obs = index.shape[1]
    total_y = n_ty * size_y
    if total_y & (total_y - 1):
        global_x = index[...] // total_y
    else:
        global_x = lax.shift_right_logical(index[...], total_y.bit_length() - 1)
    local_x = global_x - tx * size_x
    local_y = index[...] - global_x * total_y - ty * size_y
    hot[...] = jnp.where(
        lax.broadcasted_iota(jnp.int32, (size_y, n_obs), 0) == local_y, F32(1), F32(0)
    ).astype(BF16)

    for way, there, back in ((0, send_up, send_down), (1, send_down, send_up)):
        @pl.when(there)
        def _(way=way):
            for copy in row_copies(way):
                copy.wait_send()

        @pl.when(back)
        def _(way=way):
            for copy in row_copies(way):
                copy.wait_recv()
    for i, (dx, dy) in enumerate(around):
        @pl.when(inside(dx, dy))
        def _(i=i):
            edge_copy(i).wait_send()

        @pl.when(inside(-dx, -dy))
        def _(i=i):
            edge_copy(i).wait_recv()

    k_ext[...] = 0.25 * k_ext[...]

    def unpack(i):
        left, mine, right = edges[0, i], edges[1, i], edges[2, i]
        beside = jnp.where(side0, pltpu.roll(left, half, 1), pltpu.roll(right, half, 1))
        second = jnp.where(own_lane, pltpu.roll(mine, half, 1), jnp.where(side0, left, right))
        return jnp.where(own_lane, mine, beside), second

    pres, melt = unpack(0)
    elev, quarter = unpack(1)
    quarter = 0.25 * quarter
    column_global = ty * size_y + column + jnp.where(side0, -STRIP, size_y - STRIP)
    right_in = (column_global >= 0) & (column_global < n_ty * size_y - 1)

    def down_in(first, count, lanes):
        at = lax.broadcasted_iota(jnp.int32, (count, lanes), 0) + (first - PAD) + tx * size_x
        return (at >= 0) & (at < n_tx * size_x - 1)

    for t in range(SUBSTEPS):
        cond = quarter + quarter * jnp.tanh(0.5 * pres)
        head = pres + elev
        over = jnp.where(
            right_in,
            (cond + pltpu.roll(cond, 127, 1)) * (pltpu.roll(head, 127, 1) - head), F32(0),
        )
        faces[t] = over
        if t < SUBSTEPS - 1:
            down = jnp.where(
                down_in(0, rows, 128),
                (cond + pltpu.roll(cond, rows - 1, 0)) * (pltpu.roll(head, rows - 1, 0) - head),
                F32(0),
            )
            pres = pres + (over - pltpu.roll(over, 1, 1)) + (down - pltpu.roll(down, 1, 0)) + melt

    inner = list(range(PAD, PAD + size_x, CHUNK)) + [PAD + size_x]
    wide = [HALO] + inner[1:-1] + [PAD + size_x + HALO]

    def fore_copy(step, m):
        return pltpu.make_async_remote_copy(
            src_ref=fore.at[me_mem, m], dst_ref=fore.at[me_mem, m],
            send_sem=fore_send.at[step, m], recv_sem=fore_recv.at[step, m],
            device_id=partner(step),
        )

    def member(m, carry):
        for t in range(SUBSTEPS):
            cuts = wide if t < SUBSTEPS - 1 else inner
            for a, b in zip(cuts[:-1], cuts[1:]):
                count = b - a + 2 * HALO
                span = pl.ds(a - HALO, count)
                p = p_ext[m, span, :] if t == 0 else ping[(t - 1) % 2, span, :]
                k = k_ext[span, :]
                cond = k + k * jnp.tanh(0.5 * p)
                head = p + e_ext[span, :]
                down = (cond + pltpu.roll(cond, count - 1, 0)) * (
                    pltpu.roll(head, count - 1, 0) - head
                )
                if a <= PAD or b >= PAD + size_x:
                    down = jnp.where(down_in(a - HALO, count, size_y), down, F32(0))
                upright = (down - pltpu.roll(down, 1, 0))[HALO : count - HALO]
                c, h = cond[HALO : count - HALO], head[HALO : count - HALO]
                over = (c + pltpu.roll(c, size_y - 1, 1)) * (pltpu.roll(h, size_y - 1, 1) - h)
                face = faces[t, pl.ds(a, b - a), :]
                low = pltpu.roll(face, 128 - (STRIP - 1) - 8 * m, 1)
                high = pltpu.roll(face, 128 - half - STRIP - 8 * m, 1)
                over = jnp.concatenate(
                    [over[:, :-128], jnp.where(lane == 127, high, over[:, -128:])], axis=1
                )
                back = pltpu.roll(over, 1, 1)
                back = jnp.concatenate(
                    [jnp.where(lane == 0, low, back[:, :128]), back[:, 128:]], axis=1
                )
                new = (
                    p[HALO : count - HALO] + (over - back) + upright
                    + m_ext[m, pl.ds(a, b - a), :]
                )
                if t < SUBSTEPS - 1:
                    ping[t % 2, pl.ds(a, b - a), :] = new
                else:
                    out[m, pl.ds(a - PAD, b - a), :] = new
                    fore[me_mem, m, pl.ds(a - PAD, b - a), :] = new.astype(BF16)
        @pl.when(m < members - LATE)
        def _():
            for step in range(1, n_mem):
                fore_copy(step, m).start()

        value = out[m]
        top = value.astype(BF16)
        rest = (value - top.astype(F32)).astype(BF16)
        piece = 256 if n_obs % 256 == 0 else n_obs
        row = lax.broadcasted_iota(jnp.int32, (size_x, piece), 0)
        for at in range(0, n_obs, piece):
            some = hot[:, at : at + piece]
            got = jnp.dot(top, some, preferred_element_type=F32) + jnp.dot(
                rest, some, preferred_element_type=F32
            )
            got = jnp.where(row == local_x[:, at : at + piece], got, F32(0))
            picks[pl.ds(me_mem * members + m, 1), at : at + piece] = jnp.sum(
                got, axis=0, keepdims=True
            )
        return carry

    lax.fori_loop(0, members, member, 0)

    mine = pl.ds(pl.multiple_of(me_mem * members, 8), members)

    group = 16

    def pick_copy(step):
        return pltpu.make_async_remote_copy(
            src_ref=picks.at[mine, :], dst_ref=picks.at[mine, :],
            send_sem=pick_send.at[step], recv_sem=pick_recv.at[step], device_id=partner(step),
        )

    for step in range(1, n_mem):
        pick_copy(step).start()
    slabs = SLABS
    per_slab = size_x // group // slabs

    def slab_rows(i):
        return pl.ds(i * per_slab * group, per_slab * group)

    def late_copy(step, i):
        piece = fore.at[me_mem, pl.ds(members - LATE, LATE), slab_rows(i), :]
        return pltpu.make_async_remote_copy(
            src_ref=piece, dst_ref=piece, send_sem=late_send.at[step, i],
            recv_sem=late_recv.at[step, i], device_id=partner(step),
        )

    for i in range(slabs):
        for step in range(1, n_mem):
            late_copy(step, i).start()

    def obs_wait(step, carry):
        obs_copy(step).wait()
        return carry

    lax.fori_loop(1, n_plane, obs_wait, 0)
    per = 128 // share
    parts = []
    for first in range(0, n_plane, per):
        part = obs[first]
        for j in range(1, per):
            part = part + pltpu.roll(obs[first + j], j * share, 1)
        parts.append(part)
    every = jnp.concatenate(parts, axis=1)
    noise, value, error = every[:members], every[members : members + 1], every[members + 1 : members + 2]
    here = (local_x >= 0) & (local_x < size_x) & (local_y >= 0) & (local_y < size_y)

    for step in range(1, n_mem):
        pick_copy(step).wait()
    innovation = (value + error * noise - picks[mine, :]) / error
    seen = picks[...]
    anomaly = (seen - jnp.mean(seen, axis=0, keepdims=True)) / error
    anomaly = jnp.where(here, anomaly, F32(0))
    lanes = sums.shape[2]
    both = jnp.concatenate(
        [anomaly, innovation, jnp.zeros((lanes - total - members, n_obs), F32)], axis=0
    )
    sums[me] = lax.dot_general(
        anomaly, both, (((1,), (1,)), ((), ())),
        precision=lax.Precision.HIGHEST, preferred_element_type=F32,
    )

    def sum_copy(step):
        return pltpu.make_async_remote_copy(
            src_ref=sums.at[me], dst_ref=sums.at[me], send_sem=sum_send.at[step],
            recv_sem=sum_recv.at[step], device_id=plane(step),
        )

    def sum_start(step, carry):
        sum_copy(step).start()
        return carry

    def sum_wait(step, carry):
        sum_copy(step).wait()
        return carry

    lax.fori_loop(1, n_plane, sum_start, 0)
    lax.fori_loop(1, n_plane, sum_wait, 0)
    ri = lax.broadcasted_iota(jnp.int32, (total, lanes), 0)
    ci = lax.broadcasted_iota(jnp.int32, (total, lanes), 1)
    system = jnp.sum(sums[...], axis=0) + jnp.where(ri == ci, F32(total - 1), F32(0))
    for k in range(total):
        pivot = system[k : k + 1, :] / system[k : k + 1, k : k + 1]
        system = jnp.where(ri == k, pivot, system - system[:, k : k + 1] * pivot)
    weights = system.astype(BF16)

    ra = lax.broadcasted_iota(jnp.int32, (members * group, lanes), 0)
    rb = lax.broadcasted_iota(jnp.int32, (members * group, lanes), 1)
    choose = jnp.where(rb - total == ra // group, F32(1), F32(0)).astype(BF16)
    spread = lax.dot_general(
        choose, weights, (((1,), (1,)), ((), ())), preferred_element_type=F32
    ).astype(BF16)
    ca = lax.broadcasted_iota(jnp.int32, (total, total * group), 0)
    cb = lax.broadcasted_iota(jnp.int32, (total, total * group), 1)
    repeat = jnp.where(cb // group == ca, F32(1), F32(0)).astype(BF16)
    spread = jnp.dot(spread, repeat, preferred_element_type=F32)
    da = lax.broadcasted_iota(jnp.int32, spread.shape, 0)
    db = lax.broadcasted_iota(jnp.int32, spread.shape, 1)
    spread = jnp.where((da & (group - 1)) == (db & (group - 1)), spread, F32(0)).astype(BF16)

    def fore_wait(m, carry):
        for step in range(1, n_mem):
            fore_copy(step, m).wait()
        return carry

    lax.fori_loop(0, members - LATE, fore_wait, 0)

    def finish(g, carry):
        span = pl.ds(pl.multiple_of(g * group, group), group)
        block = fore[:, :, span, :].reshape(total * group, size_y)
        shift = jnp.dot(spread, block, preferred_element_type=F32)
        out[:, span, :] = out[:, span, :] + shift.reshape(members, group, size_y)
        return carry

    def leave(i):
        span = slab_rows(i)
        return pltpu.make_async_copy(out.at[:, span, :], out_hbm.at[:, span, :], load_sem.at[i])

    for i in range(slabs):
        for step in range(1, n_mem):
            late_copy(step, i).wait()
        lax.fori_loop(i * per_slab, (i + 1) * per_slab, finish, 0)
        leave(i).start()
    for i in range(slabs):
        leave(i).wait()


def local(pressure, elevation, ks_field, melt_rate, obs_index, obs_value, obs_error, perturbation):
    members, size_x, size_y = pressure.shape
    n_mem, n_tx, n_ty = (lax.axis_size(a) for a in ("mem", "tx", "ty"))
    n_plane = n_tx * n_ty
    total = n_mem * members
    share = obs_value.shape[0]
    n_obs = obs_index.shape[0]
    height = -(-(members + 2) // 8) * 8
    lanes = -(-(total + members) // 128) * 128
    rows = size_x + 2 * PAD
    dma = pltpu.SemaphoreType.DMA
    hbm = pl.BlockSpec(memory_space=pltpu.HBM)
    return pl.pallas_call(
        functools.partial(kernel, n_mem, n_tx, n_ty, share),
        out_shape=jax.ShapeDtypeStruct(pressure.shape, F32),
        in_specs=[hbm] * 8,
        out_specs=hbm,
        scratch_shapes=[
            pltpu.VMEM(pressure.shape, F32),
            pltpu.VMEM((members, rows, size_y), F32),
            pltpu.VMEM((members, rows, size_y), F32),
            pltpu.VMEM((rows, size_y), F32),
            pltpu.VMEM((rows, size_y), F32),
            pltpu.VMEM((2, rows, size_y), F32),
            pltpu.VMEM((3, 2, rows, 128), F32),
            pltpu.VMEM((SUBSTEPS, rows, 128), F32),
            pltpu.VMEM((size_y, n_obs), BF16),
            pltpu.VMEM((n_mem, members, size_x, size_y), BF16),
            pltpu.VMEM((n_plane, height, 128), F32),
            pltpu.VMEM((total, n_obs), F32),
            pltpu.VMEM((n_plane, total, lanes), F32),
            pltpu.VMEM((1, n_obs), jnp.int32),
            pltpu.VMEM((1, share), F32),
            pltpu.VMEM((1, share), F32),
            pltpu.VMEM((members, share), F32),
            dma((8,)), dma((2, 4)), dma((2, 4)), dma((8,)), dma((8,)),
            dma((n_plane,)), dma((n_plane,)),
            dma((n_mem, members)), dma((n_mem, members)),
            dma((n_mem, SLABS)), dma((n_mem, SLABS)),
            dma((n_mem,)), dma((n_mem,)), dma((n_plane,)), dma((n_plane,)),
        ],
        compiler_params=pltpu.CompilerParams(
            collective_id=0, has_side_effects=True, vmem_limit_bytes=57 * 2**20
        ),
    )(
        pressure, elevation, ks_field, melt_rate,
        obs_index[None], obs_value[None], obs_error[None], perturbation.T,
    )


def solution(mesh):
    placed = (
        P("mem", "tx", "ty"),
        P("tx", "ty"),
        P("tx", "ty"),
        P("mem", "tx", "ty"),
        P(),
        P(("tx", "ty")),
        P(("tx", "ty")),
        P(("tx", "ty"), "mem"),
    )
    return jax.shard_map(
        local, mesh=mesh, in_specs=placed, out_specs=P("mem", "tx", "ty"), check_vma=False
    )
```
